512 devices in a mesh: dp: 64 (over y, x, z_lo), tensor: 8 (over z_hi, core).
Axes of the slice: x: 4, y: 4, z: 16 (z_hi: 4, z_lo: 4; z = z_hi * 4 + z_lo), core: 2. Of those that a mesh axis runs over, the one named last changes fastest.
Arguments:
- grad_out: bfloat16 [16384, 4096], P('dp'), may hold values from -4 to 4
- hidden: bfloat16 [16384, 11008], P('dp', 'tensor'), may hold values from -6 to 6
- proj_basis: bfloat16 [4096, 512], P('dp'), may hold values from -0.09375 to 0.09375
- weight: bfloat16 [4096, 11008], P('dp', 'tensor'), may hold values from -0.75 to 0.75
- first_moment: float32 [512, 11008], P('dp', 'tensor'), may hold values from -6 to 6
- second_moment: float32 [512, 11008], P('dp', 'tensor'), may hold values from 0.5 to 4
Outputs:
- new_weight: bfloat16 [4096, 11008], P('dp')
- new_first: float32 [512, 11008], P('dp', 'tensor')
- new_second: float32 [512, 11008], P('dp', 'tensor')
The draws below stay inside these ranges and needn't reach their ends.
All inputs are finite; a program needn't handle non-finite values.
Results may differ from the reference program's by a relative error of at most 0.0053.
Values may be sent and summed in bfloat16 or wider, within the bound.
A program may use at most 64 MiB of HBM per device.

```python
import math
import jax
import jax.numpy as jnp

D = 4096
FF = 11008
RANK = 512
TOKENS = 16384


def shard_levels(key, shape, shards, least, largest):
    factor_of = 1.0
    for dim, shards_of in shards:
        heights = jax.random.uniform(jax.random.fold_in(jax.random.fold_in(key, 6), dim), (shards_of,), jnp.float32, least / len(shards), largest / len(shards))
        factor_of = factor_of * jnp.repeat(jnp.exp(heights), shape[dim] // shards_of).reshape((-1,) + (1,) * (len(shape) - 1 - dim))
    return factor_of


def scatter_about(key, shape, scale, reach, shards=(), held_as=jnp.bfloat16):
    result = jax.random.normal(key, shape, jnp.float32) * scale
    if len(shards) > 0:
        result = shard_levels(key, shape, shards, -0.22, 0.18) * result
    return jnp.clip(result, min=-reach, max=reach).astype(held_as)


def setup_inputs(seed: int = 0) -> dict:
    seeds = jax.random.split(jax.random.key(seed), 7)
    grad_out = scatter_about(seeds[0], (TOKENS, D), 0.25, 4.0, ((0, 64),))
    hidden = scatter_about(seeds[1], (TOKENS, FF), 1.0, 6.0, ((0, 64), (1, 8)))
    proj_basis = scatter_about(seeds[2], (D, RANK), D ** -0.5, 0.09375, ((0, 64),))
    weight = scatter_about(seeds[3], (D, FF), 0.05, 0.75, ((0, 64), (1, 8)))
    first_moment = scatter_about(seeds[4], (RANK, FF), 1.0, 6.0, ((0, 64), (1, 8)), jnp.float32)
    second_moment = jnp.clip(jnp.exp(math.log(4.0) - 2.0794415 * jax.random.uniform(seeds[5], (RANK, FF), jnp.float32) ** shard_levels(seeds[5], (RANK, FF), ((0, 64), (1, 8)), -0.2, 0.2)), 0.5, 4.0)
    return {"grad_out": grad_out, "hidden": hidden, "proj_basis": proj_basis, "weight": weight, "first_moment": first_moment, "second_moment": second_moment}


def reference(grad_out, hidden, proj_basis, weight, first_moment, second_moment):
    projected = jnp.dot(grad_out, proj_basis, preferred_element_type=jnp.float32).astype(jnp.bfloat16)
    grad_low = jnp.dot(projected.T, hidden, preferred_element_type=jnp.float32)
    new_first = 0.9 * first_moment + 0.1 * grad_low
    new_second = 0.999 * second_moment + 0.001 * grad_low * grad_low
    direction = (new_first / (jnp.sqrt(new_second) + 1e-08)).astype(jnp.bfloat16)
    update = jnp.dot(proj_basis, direction, preferred_element_type=jnp.float32)
    new_weight = (weight.astype(jnp.float32) - 0.1 * update).astype(jnp.bfloat16)
    return (new_weight, new_first, new_second)
```

```python
import functools

import jax
import jax.numpy as jnp
from jax import lax
from jax.experimental import pallas as pl
from jax.experimental.pallas import tpu as pltpu
from jax.sharding import PartitionSpec as P

MESH = pl.DeviceIdType.MESH
F32 = jnp.float32
BF16 = jnp.bfloat16

WIDTH = 1376
CHUNKS = ((0, 512, 512), (512, 512, 512), (1024, 352, 384))
HALF = 256
SLOT = 1408


def pack(rows):
    low, high = rows[:, :HALF], rows[:, HALF:]
    if high.shape[1] < HALF:
        high = jnp.concatenate(
            [high, jnp.zeros((8, HALF - high.shape[1]), high.dtype)], axis=1
        )
    return jnp.concatenate([low, high], axis=0)


def unpack(block):
    return jnp.concatenate([block[:8], block[8:]], axis=1)


def kernel(
    grad_ref, hidden_ref, basis_ref, weight_ref, first_ref, second_ref,
    slots_ref, new_first_ref, new_second_ref,
    grad, hidden, basis, weight, first, second, load_sem,
    gathered, expand, proj, dirs,
    part0, part1, part2, ra0, ra1, ra2, sa0, sa1, sa2, rb0, rb1, rb2,
    sz, szf, rz, steps, local_new, own_sem,
    a_send, a_recv, p_send, p_recv, c_send, c_recv,
):
    parts, ras, sas, rbs = (part0, part1, part2), (ra0, ra1, ra2), (sa0, sa1, sa2), (rb0, rb1, rb2)
    dp, tensor = lax.axis_index("dp"), lax.axis_index("tensor")
    y, x, z = dp // 16, (dp // 4) % 4, dp % 4
    hi, core = tensor // 2, tensor % 2
    even = core == 0
    a, b = jnp.where(even, y, x), jnp.where(even, x, y)

    def device(a_, b_, z_, hi_, core_):
        y_, x_ = jnp.where(even, a_, b_), jnp.where(even, b_, a_)
        return ((y_ * 4 + x_) * 4 + z_, hi_ * 2 + core_)

    a_peers = [device((a + k) % 4, b, z, hi, core) for k in (1, 2, 3)]
    b_peers = [device(a, (b + k) % 4, z, hi, core) for k in (1, 2, 3)]
    z_peers = [device(a, b, (z + k) % 4, hi, core) for k in (1, 2, 3)]
    hi_next = device(a, b, z, (hi + 1) % 4, core)
    hi_prev = device(a, b, z, (hi + 3) % 4, core)
    sibling = (dp, hi * 2 + 1 - core)

    loads = [
        pltpu.make_async_copy(basis_ref, basis, load_sem.at[0]),
        pltpu.make_async_copy(grad_ref, grad, load_sem.at[1]),
        pltpu.make_async_copy(hidden_ref, hidden.at[pl.ds(0, WIDTH)], load_sem.at[2]),
        pltpu.make_async_copy(first_ref, first, load_sem.at[3]),
        pltpu.make_async_copy(second_ref, second, load_sem.at[4]),
        pltpu.make_async_copy(weight_ref, weight, load_sem.at[5]),
    ]
    for load in loads:
        load.start()

    barrier = pltpu.get_barrier_semaphore()
    friends = a_peers + b_peers + z_peers + [hi_next, hi_prev, sibling]
    for friend in friends:
        pl.semaphore_signal(barrier, inc=1, device_id=friend, device_id_type=MESH)

    sends = []

    def send(src, dst, send_sem, recv_sem, to):
        copy = pltpu.make_async_remote_copy(
            src_ref=src, dst_ref=dst, send_sem=send_sem, recv_sem=recv_sem,
            device_id=to, device_id_type=MESH,
        )
        copy.start()
        sends.append(copy)
        return copy

    hidden[pl.ds(WIDTH, SLOT - WIDTH)] = jnp.zeros((SLOT - WIDTH, 256), BF16)
    dirs[...] = jnp.zeros_like(dirs)
    loads[0].wait()
    mine = a * 16 + b * 4 + z
    columns = pl.ds(pl.multiple_of(core * 256, 256), 256)
    gathered[mine] = basis[:, columns]
    pl.semaphore_wait(barrier, len(friends))

    wait_z = [send(gathered.at[mine], gathered.at[mine], a_send.at[k], a_recv.at[k], z_peers[k]) for k in range(3)]

    lane = lax.broadcasted_iota(jnp.int32, (512, 1024), 1)
    row = lax.broadcasted_iota(jnp.int32, (512, 1024), 0)
    la, lb = lane // 256, (lane // 64) % 4
    rank = jnp.where(even, la * 4 + lb, lb * 4 + la) * 32 + (lane // 16 % 4) * 8 + lane % 8
    spread = jnp.dot(
        basis[...], jnp.where(row == rank, 1.0, 0.0).astype(BF16), preferred_element_type=F32
    )
    lower = lax.broadcasted_iota(jnp.int32, (64, 1024), 1) // 8 % 2 == 0
    expand[0] = jnp.where(lower, spread, 0.0).astype(BF16)
    expand[1] = jnp.where(lower, 0.0, spread).astype(BF16)

    for copy in wait_z:
        copy.wait_recv()
    block = pl.ds(a * 16 + b * 4, 4)
    wait_b = [send(gathered.at[block], gathered.at[block], a_send.at[3 + k], a_recv.at[3 + k], b_peers[k]) for k in range(3)]
    for copy in wait_b:
        copy.wait_recv()
    block = pl.ds(a * 16, 16)
    wait_a = [send(gathered.at[block], gathered.at[block], a_send.at[6 + k], a_recv.at[6 + k], a_peers[k]) for k in range(3)]
    loads[1].wait()

    def project(total, a_):
        for b_ in range(4):
            at = pl.multiple_of(jnp.where(even, a_ * 4 + b_, b_ * 4 + a_) * 256, 256)
            rows = gathered[pl.ds(a_ * 16 + b_ * 4, 4)].reshape(256, 256)
            total += jnp.dot(grad[:, pl.ds(at, 256)], rows, preferred_element_type=F32)
        return total

    total = project(jnp.zeros((256, 256), F32), a)
    for k in (0, 2, 1):
        wait_a[k].wait_recv()
        total = project(total, (a + 3 - k) % 4)
    proj[core] = total.T.astype(BF16)
    half = send(proj.at[core], proj.at[core], p_send, p_recv, sibling)
    loads[2].wait()
    half.wait_recv()
    for load in loads[3:]:
        load.wait()

    waits = {}

    def stage_partial(c):
        first_column, _, padded = CHUNKS[c]
        for h in range(2):
            part = lax.dot_general(
                proj[h], hidden[pl.ds(first_column, padded)],
                (((1,), (1,)), ((), ())), preferred_element_type=F32,
            )
            for i in range(8):
                y_, x_ = (h * 8 + i) // 4, i % 4
                parts[c][jnp.where(even, y_ * 4 + x_, x_ * 4 + y_)] = part[i * 32 : i * 32 + 32].astype(BF16)
        waits["a", c] = [
            send(parts[c].at[pl.ds((a + k + 1) % 4 * 4, 4)], ras[c].at[k], c_send.at[c, k], c_recv.at[c, k], a_peers[k])
            for k in range(3)
        ]

    def stage_sum_a(c):
        for copy in waits["a", c]:
            copy.wait_recv()
        total = parts[c][pl.ds(a * 4, 4)].astype(F32)
        for k in range(3):
            total += ras[c][k].astype(F32)
        sas[c][...] = total.astype(BF16)
        waits["b", c] = [
            send(sas[c].at[(b + k + 1) % 4], rbs[c].at[k], c_send.at[c, 3 + k], c_recv.at[c, 3 + k], b_peers[k])
            for k in range(3)
        ]

    def stage_sum_b(c):
        padded = CHUNKS[c][2]
        total = parts[c][a * 4 + b].astype(F32)
        for k in range(3):
            total += ras[c][k, b].astype(F32)
        for copy in waits["b", c]:
            copy.wait_recv()
        for k in range(3):
            total += rbs[c][k].astype(F32)
        for z_ in range(4):
            block = pack(total[z_ * 8 : z_ * 8 + 8])
            szf[c, z_] = block
            sz[c, z_] = block.astype(BF16)
        waits["z", c] = [
            send(sz.at[c, (z + k + 1) % 4], rz.at[c, k], c_send.at[c, 6 + k], c_recv.at[c, 6 + k], z_peers[k])
            for k in range(3)
        ]

    def stage_moments(c):
        first_column, valid, _ = CHUNKS[c]
        at = pl.ds(first_column, valid)
        for copy in waits["z", c]:
            copy.wait_recv()
        total = szf[c, z]
        for k in range(3):
            total += rz[c, k].astype(F32)
        grad_low = unpack(total)[:, :valid]
        new_first = 0.9 * first[:, at] + 0.1 * grad_low
        new_second = 0.999 * second[:, at] + 0.001 * grad_low * grad_low
        new_first_ref[:, at] = new_first
        new_second_ref[:, at] = new_second
        dirs[:, at] = new_first / (jnp.sqrt(new_second) + 1e-08)
        steps[c, mine] = pack(dirs[:, pl.ds(first_column, 512)]).astype(BF16)
        waits["gz", c] = [
            send(steps.at[c, mine], steps.at[c, mine], c_send.at[c, 9 + k], c_recv.at[c, 9 + k], z_peers[k])
            for k in range(3)
        ]

    def stage_gather_b(c):
        for copy in waits["gz", c]:
            copy.wait_recv()
        block = pl.ds(a * 16 + b * 4, 4)
        waits["gb", c] = [
            send(steps.at[c, block], steps.at[c, block], c_send.at[c, 12 + k], c_recv.at[c, 12 + k], b_peers[k])
            for k in range(3)
        ]

    def stage_gather_a(c):
        for copy in waits["gb", c]:
            copy.wait_recv()
        block = pl.ds(a * 16, 16)
        waits["ga", c] = [
            send(steps.at[c, block], steps.at[c, block], c_send.at[c, 15 + k], c_recv.at[c, 15 + k], a_peers[k])
            for k in range(3)
        ]

    def slot(c, hi_, core_, rows=pl.ds(0, 64)):
        return slots_ref.at[hi_ * 2 + core_, rows, pl.ds(CHUNKS[c][0], CHUNKS[c][2])]

    top, bottom = pl.ds(0, 32), pl.ds(32, 32)
    own = []

    def stage_update(c):
        first_column, valid, padded = CHUNKS[c]
        for copy in waits["ga", c]:
            copy.wait_recv()
        every = steps[c].reshape(1024, HALF)
        update = jnp.concatenate(
            [jnp.dot(expand[h], every, preferred_element_type=F32) for h in range(2)], axis=1
        )[:, :valid]
        new = weight[:, pl.ds(first_column, valid)].astype(F32) - 0.1 * update
        local_new[:, pl.ds(first_column, valid)] = new.astype(BF16)
        src = local_new.at[:, pl.ds(first_column, padded)]
        waits["n", c] = send(src, slot(c, hi, core), c_send.at[c, 18], c_recv.at[c, 18], hi_next)
        waits["p", c] = send(src, slot(c, hi, core), c_send.at[c, 19], c_recv.at[c, 19], hi_prev)
        waits["s", c] = send(src, slot(c, hi, core), c_send.at[c, 20], c_recv.at[c, 20], sibling)
        copy = pltpu.make_async_copy(src, slot(c, hi, core), own_sem.at[c])
        copy.start()
        own.append(copy)

    def stage_forward(c):
        waits["n", c].wait_recv()
        prev = (hi + 3) % 4
        waits["n2", c] = send(slot(c, prev, core, top), slot(c, prev, core, top), c_send.at[c, 21], c_recv.at[c, 21], hi_next)
        waits["ns", c] = send(slot(c, prev, core), slot(c, prev, core), c_send.at[c, 22], c_recv.at[c, 22], sibling)
        waits["p", c].wait_recv()
        following = (hi + 1) % 4
        waits["p2", c] = send(slot(c, following, core, bottom), slot(c, following, core, bottom), c_send.at[c, 23], c_recv.at[c, 23], hi_prev)
        waits["ps", c] = send(slot(c, following, core), slot(c, following, core), c_send.at[c, 24], c_recv.at[c, 24], sibling)

    def stage_finish(c):
        far = (hi + 2) % 4
        waits["n2", c].wait_recv()
        waits["fs", c] = send(slot(c, far, core, top), slot(c, far, core, top), c_send.at[c, 25], c_recv.at[c, 25], sibling)
        waits["p2", c].wait_recv()
        waits["gs", c] = send(slot(c, far, core, bottom), slot(c, far, core, bottom), c_send.at[c, 26], c_recv.at[c, 26], sibling)

    stages = (
        stage_partial, stage_sum_a, stage_sum_b, stage_moments, stage_gather_b,
        stage_gather_a, stage_update, stage_forward, stage_finish,
    )
    n = len(CHUNKS)
    for step in range(len(stages) + n - 1):
        for c in range(n):
            if 0 <= step - c < len(stages):
                stages[step - c](c)
    for c in range(n):
        for name in ("s", "ns", "ps", "fs", "gs"):
            waits[name, c].wait_recv()
    for copy in own:
        copy.wait()
    for copy in sends:
        copy.wait_send()


def local(grad_out, hidden, proj_basis, weight, first_moment, second_moment):
    n = len(CHUNKS)
    wide = [padded for _, _, padded in CHUNKS]
    hbm = pl.BlockSpec(memory_space=pl.ANY)
    vmem = pl.BlockSpec(memory_space=pltpu.VMEM)
    dma = pltpu.SemaphoreType.DMA
    slots, new_first, new_second = pl.pallas_call(
        kernel,
        name="step",
        out_shape=(
            jax.ShapeDtypeStruct((8, 64, SLOT), BF16),
            jax.ShapeDtypeStruct((8, WIDTH), F32),
            jax.ShapeDtypeStruct((8, WIDTH), F32),
        ),
        in_specs=[hbm] * 6,
        out_specs=(hbm, vmem, vmem),
        scratch_shapes=[
            pltpu.VMEM((256, 4096), BF16),
            pltpu.VMEM((SLOT, 256), BF16),
            pltpu.VMEM((64, 512), BF16),
            pltpu.VMEM((64, WIDTH), BF16),
            pltpu.VMEM((8, WIDTH), F32),
            pltpu.VMEM((8, WIDTH), F32),
            dma((6,)),
            pltpu.VMEM((64, 64, 256), BF16),
            pltpu.VMEM((2, 64, 1024), BF16),
            pltpu.VMEM((2, 256, 256), BF16),
            pltpu.VMEM((8, 1536), F32),
            *[pltpu.VMEM((16, 32, w), BF16) for w in wide],
            *[pltpu.VMEM((3, 4, 32, w), BF16) for w in wide],
            *[pltpu.VMEM((4, 32, w), BF16) for w in wide],
            *[pltpu.VMEM((3, 32, w), BF16) for w in wide],
            pltpu.VMEM((n, 4, 16, HALF), BF16),
            pltpu.VMEM((n, 4, 16, HALF), F32),
            pltpu.VMEM((n, 3, 16, HALF), BF16),
            pltpu.VMEM((n, 64, 16, HALF), BF16),
            pltpu.VMEM((64, SLOT), BF16),
            dma((n,)),
            dma((9,)), dma((9,)), dma, dma, dma((n, 27)), dma((n, 27)),
        ],
        compiler_params=pltpu.CompilerParams(
            collective_id=0, has_side_effects=True, vmem_limit_bytes=40 * 2**20
        ),
    )(grad_out, hidden.T, proj_basis, weight, first_moment, second_moment)
    new_weight = jnp.concatenate([slots[t, :, :WIDTH] for t in range(8)], axis=1)
    return (new_weight, new_first, new_second)


def solution(mesh):
    return jax.shard_map(
        local,
        mesh=mesh,
        in_specs=(
            P("dp", None),
            P("dp", "tensor"),
            P("dp", None),
            P("dp", "tensor"),
            P("dp", "tensor"),
            P("dp", "tensor"),
        ),
        out_specs=(P("dp", None), P("dp", "tensor"), P("dp", "tensor")),
        check_vma=False,
    )
```

```python
import functools

import jax
import jax.numpy as jnp
from jax import lax
from jax.experimental import pallas as pl
from jax.experimental.pallas import tpu as pltpu
from jax.sharding import PartitionSpec as P

MESH = pl.DeviceIdType.MESH
F32 = jnp.float32
BF16 = jnp.bfloat16

WIDTH = 1376
CHUNKS = ((0, 512, 512), (512, 512, 512), (1024, 352, 384))
HALF = 256
SLOT = 1408
ORDER = "P0 P1 S0 P2 M0 S1 G0 M1 S2 U0 G1 M2 U1 F0 G2 U2 F1 E0 F2 E1 E2"


def pack(rows):
    low, high = rows[:, :HALF], rows[:, HALF:]
    if high.shape[1] < HALF:
        high = jnp.concatenate(
            [high, jnp.zeros((8, HALF - high.shape[1]), high.dtype)], axis=1
        )
    return jnp.concatenate([low, high], axis=0)


def unpack(block):
    return jnp.concatenate([block[:8], block[8:]], axis=1)


def kernel(
    grad_ref, hidden_ref, basis_ref, weight_ref, first_ref, second_ref,
    slots_ref, new_first_ref, new_second_ref,
    grad, hidden, basis, weight, first, second, load_sem,
    gathered, expand, proj, dirs,
    part0, part1, part2, ra0, ra1, ra2, sz, rz, steps, local_new, own_sem,
    a_send, a_recv, p_send, p_recv, c_send, c_recv,
):
    parts, ras = (part0, part1, part2), (ra0, ra1, ra2)
    dp, tensor = lax.axis_index("dp"), lax.axis_index("tensor")
    y, x, z = dp // 16, (dp // 4) % 4, dp % 4
    hi, core = tensor // 2, tensor % 2
    even = core == 0
    a, b = jnp.where(even, y, x), jnp.where(even, x, y)

    def device(a_, b_, z_, hi_, core_):
        y_, x_ = jnp.where(even, a_, b_), jnp.where(even, b_, a_)
        return ((y_ * 4 + x_) * 4 + z_, hi_ * 2 + core_)

    a_peers = [device((a + k) % 4, b, z, hi, core) for k in (1, 2, 3)]
    b_peers = [device(a, (b + k) % 4, z, hi, core) for k in (1, 2, 3)]
    z_peers = [device(a, b, (z + k) % 4, hi, core) for k in (1, 2, 3)]
    hi_next = device(a, b, z, (hi + 1) % 4, core)
    hi_prev = device(a, b, z, (hi + 3) % 4, core)
    sibling = (dp, hi * 2 + 1 - core)

    loads = [
        pltpu.make_async_copy(basis_ref, basis, load_sem.at[0]),
        pltpu.make_async_copy(grad_ref, grad, load_sem.at[1]),
        pltpu.make_async_copy(hidden_ref, hidden.at[pl.ds(0, WIDTH)], load_sem.at[2]),
        pltpu.make_async_copy(first_ref, first, load_sem.at[3]),
        pltpu.make_async_copy(second_ref, second, load_sem.at[4]),
        pltpu.make_async_copy(weight_ref, weight, load_sem.at[5]),
    ]
    for load in loads:
        load.start()

    barrier = pltpu.get_barrier_semaphore()
    friends = a_peers + b_peers + z_peers + [hi_next, hi_prev, sibling]
    for friend in friends:
        pl.semaphore_signal(barrier, inc=1, device_id=friend, device_id_type=MESH)

    sends = []

    def send(src, dst, send_sem, recv_sem, to):
        copy = pltpu.make_async_remote_copy(
            src_ref=src, dst_ref=dst, send_sem=send_sem, recv_sem=recv_sem,
            device_id=to, device_id_type=MESH,
        )
        copy.start()
        sends.append(copy)
        return copy

    hidden[pl.ds(WIDTH, SLOT - WIDTH)] = jnp.zeros((SLOT - WIDTH, 256), BF16)
    dirs[...] = jnp.zeros_like(dirs)
    loads[0].wait()
    mine = a * 16 + b * 4 + z
    columns = pl.ds(pl.multiple_of(core * 256, 256), 256)
    gathered[mine] = basis[:, columns]
    pl.semaphore_wait(barrier, len(friends))

    near = (1, 3, 2)
    arrivals = {}

    def pass_on(kb, kz, axes):
        at = gathered.at[a * 16 + (b + 4 - kb) % 4 * 4 + (z + 4 - kz) % 4]
        for axis in axes:
            for k in near:
                if axis == "z":
                    index, to, key = k - 1, z_peers[k - 1], (0, 0, k)
                elif axis == "b":
                    index, to, key = 3 + kz * 3 + k - 1, b_peers[k - 1], (0, k, kz)
                else:
                    index, to, key = 15 + (kb * 4 + kz) * 3 + k - 1, a_peers[k - 1], (k, kb, kz)
                arrivals[key] = send(at, at, a_send.at[index], a_recv.at[index], to)

    pass_on(0, 0, "zba")
    for kz in near:
        arrivals[0, 0, kz].wait_recv()
        pass_on(0, kz, "ba")
    for kz in (0,) + near:
        for kb in near:
            arrivals[0, kb, kz].wait_recv()
            pass_on(kb, kz, "a")

    lane = lax.broadcasted_iota(jnp.int32, (1, 1024), 1)
    la, lb = lane // 256, (lane // 64) % 4
    rank = jnp.where(even, la * 4 + lb, lb * 4 + la) * 32 + (lane // 16 % 4) * 8 + lane % 8
    row = lax.broadcasted_iota(jnp.int32, (512, 1024), 0)
    spread = jnp.dot(
        basis[...], jnp.where(row == rank, 1.0, 0.0).astype(BF16), preferred_element_type=F32
    )
    lower = lane // 8 % 2 == 0
    expand[0] = jnp.where(lower, spread, 0.0).astype(BF16)
    expand[1] = jnp.where(lower, 0.0, spread).astype(BF16)
    loads[1].wait()

    total = jnp.zeros((256, 256), F32)
    for kb in (0,) + near:
        for ka in (0,) + near:
            if ka:
                for kz in range(4):
                    arrivals[ka, kb, kz].wait_recv()
            a_, b_ = (a + 4 - ka) % 4, (b + 4 - kb) % 4
            at = pl.multiple_of(jnp.where(even, a_ * 4 + b_, b_ * 4 + a_) * 256, 256)
            rows = gathered[pl.ds(a_ * 16 + b_ * 4, 4)].reshape(256, 256)
            total += jnp.dot(grad[:, pl.ds(at, 256)], rows, preferred_element_type=F32)
    proj[core] = total.T.astype(BF16)
    half = send(proj.at[core], proj.at[core], p_send, p_recv, sibling)
    loads[2].wait()
    half.wait_recv()
    for load in loads[3:]:
        load.wait()

    waits = {}

    def stage_partial(c):
        first_column, _, padded = CHUNKS[c]
        for h in range(2):
            part = lax.dot_general(
                proj[h], hidden[pl.ds(first_column, padded)],
                (((1,), (1,)), ((), ())), preferred_element_type=F32,
            )
            for i in range(8):
                y_, x_ = (h * 8 + i) // 4, i % 4
                parts[c][jnp.where(even, y_ * 4 + x_, x_ * 4 + y_)] = part[i * 32 : i * 32 + 32].astype(BF16)
        waits["a", c] = [
            send(parts[c].at[pl.ds((a + k + 1) % 4 * 4, 4)], ras[c].at[k], c_send.at[c, k], c_recv.at[c, k], a_peers[k])
            for k in range(3)
        ]

    def stage_sum_a(c):
        for copy in waits["a", c]:
            copy.wait_recv()
        total = parts[c][pl.ds(a * 4, 4)].astype(F32)
        for k in range(3):
            total += ras[c][k].astype(F32)
        for b_ in range(4):
            for z_ in range(4):
                sz[c, b_ * 4 + z_] = pack(total[b_, z_ * 8 : z_ * 8 + 8]).astype(BF16)
        waits["bz", c] = [
            send(sz.at[c, (b + kb) % 4 * 4 + (z + kz) % 4], rz.at[c, kb * 4 + kz],
                 c_send.at[c, 2 + kb * 4 + kz], c_recv.at[c, 2 + kb * 4 + kz], device(a, (b + kb) % 4, (z + kz) % 4, hi, core))
            for kb in range(4) for kz in range(4) if kb or kz
        ]

    def stage_moments(c):
        first_column, valid, _ = CHUNKS[c]
        at = pl.ds(first_column, valid)
        total = sz[c, b * 4 + z].astype(F32)
        for copy in waits["bz", c]:
            copy.wait_recv()
        for k in range(1, 16):
            total += rz[c, k].astype(F32)
        grad_low = unpack(total)[:, :valid]
        new_first = 0.9 * first[:, at] + 0.1 * grad_low
        new_second = 0.999 * second[:, at] + 0.001 * grad_low * grad_low
        new_first_ref[:, at] = new_first
        new_second_ref[:, at] = new_second
        dirs[:, at] = new_first / (jnp.sqrt(new_second) + 1e-08)
        steps[c, mine] = pack(dirs[:, pl.ds(first_column, 512)]).astype(BF16)
        waits["gz", c] = [
            send(steps.at[c, mine], steps.at[c, mine], c_send.at[c, 18 + k], c_recv.at[c, 18 + k], z_peers[k])
            for k in range(3)
        ]

    def stage_gather(c):
        for copy in waits["gz", c]:
            copy.wait_recv()
        block = steps.at[c, pl.ds(a * 16 + b * 4, 4)]
        waits["ga", c] = [
            send(block, block, c_send.at[c, 20 + ka * 4 + kb], c_recv.at[c, 20 + ka * 4 + kb], device((a + ka) % 4, (b + kb) % 4, z, hi, core))
            for ka in range(4) for kb in range(4) if ka or kb
        ]

    def slot(c, hi_, core_, rows=pl.ds(0, 64)):
        return slots_ref.at[hi_ * 2 + core_, rows, pl.ds(CHUNKS[c][0], CHUNKS[c][2])]

    top, bottom = pl.ds(0, 32), pl.ds(32, 32)
    own = []

    def stage_update(c):
        first_column, valid, padded = CHUNKS[c]
        for copy in waits["ga", c]:
            copy.wait_recv()
        every = steps[c].reshape(1024, HALF)
        update = jnp.concatenate(
            [jnp.dot(expand[h], every, preferred_element_type=F32) for h in range(2)], axis=1
        )[:, :valid]
        new = weight[:, pl.ds(first_column, valid)].astype(F32) - 0.1 * update
        local_new[:, pl.ds(first_column, valid)] = new.astype(BF16)
        src = local_new.at[:, pl.ds(first_column, padded)]
        waits["n", c] = send(src, slot(c, hi, core), c_send.at[c, 36], c_recv.at[c, 36], hi_next)
        waits["p", c] = send(src, slot(c, hi, core), c_send.at[c, 37], c_recv.at[c, 37], hi_prev)
        waits["s", c] = send(src, slot(c, hi, core), c_send.at[c, 38], c_recv.at[c, 38], sibling)
        copy = pltpu.make_async_copy(src, slot(c, hi, core), own_sem.at[c])
        copy.start()
        own.append(copy)

    def stage_forward(c):
        waits["n", c].wait_recv()
        prev = (hi + 3) % 4
        waits["n2", c] = send(slot(c, prev, core, top), slot(c, prev, core, top), c_send.at[c, 39], c_recv.at[c, 39], hi_next)
        waits["ns", c] = send(slot(c, prev, core), slot(c, prev, core), c_send.at[c, 40], c_recv.at[c, 40], sibling)
        waits["p", c].wait_recv()
        following = (hi + 1) % 4
        waits["p2", c] = send(slot(c, following, core, bottom), slot(c, following, core, bottom), c_send.at[c, 41], c_recv.at[c, 41], hi_prev)
        waits["ps", c] = send(slot(c, following, core), slot(c, following, core), c_send.at[c, 42], c_recv.at[c, 42], sibling)

    def stage_finish(c):
        far = (hi + 2) % 4
        waits["n2", c].wait_recv()
        waits["fs", c] = send(slot(c, far, core, top), slot(c, far, core, top), c_send.at[c, 43], c_recv.at[c, 43], sibling)
        waits["p2", c].wait_recv()
        waits["gs", c] = send(slot(c, far, core, bottom), slot(c, far, core, bottom), c_send.at[c, 44], c_recv.at[c, 44], sibling)

    stages = dict(
        P=stage_partial, S=stage_sum_a, M=stage_moments, G=stage_gather, U=stage_update, F=stage_forward, E=stage_finish
    )
    for item in ORDER.split():
        stages[item[0]](int(item[1]))
    n = len(CHUNKS)
    for c in range(n):
        for name in ("s", "ns", "ps", "fs", "gs"):
            waits[name, c].wait_recv()
    for copy in own:
        copy.wait()
    for copy in sends:
        copy.wait_send()


def local(grad_out, hidden, proj_basis, weight, first_moment, second_moment):
    n = len(CHUNKS)
    wide = [padded for _, _, padded in CHUNKS]
    hbm = pl.BlockSpec(memory_space=pl.ANY)
    vmem = pl.BlockSpec(memory_space=pltpu.VMEM)
    dma = pltpu.SemaphoreType.DMA
    slots, new_first, new_second = pl.pallas_call(
        kernel,
        name="step",
        out_shape=(
            jax.ShapeDtypeStruct((8, 64, SLOT), BF16),
            jax.ShapeDtypeStruct((8, WIDTH), F32),
            jax.ShapeDtypeStruct((8, WIDTH), F32),
        ),
        in_specs=[hbm] * 6,
        out_specs=(hbm, vmem, vmem),
        scratch_shapes=[
            pltpu.VMEM((256, 4096), BF16),
            pltpu.VMEM((SLOT, 256), BF16),
            pltpu.VMEM((64, 512), BF16),
            pltpu.VMEM((64, WIDTH), BF16),
            pltpu.VMEM((8, WIDTH), F32),
            pltpu.VMEM((8, WIDTH), F32),
            dma((6,)),
            pltpu.VMEM((64, 64, 256), BF16),
            pltpu.VMEM((2, 64, 1024), BF16),
            pltpu.VMEM((2, 256, 256), BF16),
            pltpu.VMEM((8, 1536), F32),
            *[pltpu.VMEM((16, 32, w), BF16) for w in wide],
            *[pltpu.VMEM((3, 4, 32, w), BF16) for w in wide],
            pltpu.VMEM((n, 16, 16, HALF), BF16),
            pltpu.VMEM((n, 16, 16, HALF), BF16),
            pltpu.VMEM((n, 64, 16, HALF), BF16),
            pltpu.VMEM((64, SLOT), BF16),
            dma((n,)),
            dma((63,)), dma((63,)), dma, dma, dma((n, 45)), dma((n, 45)),
        ],
        compiler_params=pltpu.CompilerParams(
            collective_id=0, has_side_effects=True, vmem_limit_bytes=62 * 2**20
        ),
    )(grad_out, hidden.T, proj_basis, weight, first_moment, second_moment)
    new_weight = jnp.concatenate([slots[t, :, :WIDTH] for t in range(8)], axis=1)
    return (new_weight, new_first, new_second)


def solution(mesh):
    return jax.shard_map(
        local,
        mesh=mesh,
        in_specs=(
            P("dp", None),
            P("dp", "tensor"),
            P("dp", None),
            P("dp", "tensor"),
            P("dp", "tensor"),
            P("dp", "tensor"),
        ),
        out_specs=(P("dp", None), P("dp", "tensor"), P("dp", "tensor")),
        check_vma=False,
    )
```

```python
import functools

import jax
import jax.numpy as jnp
from jax import lax
from jax.experimental import pallas as pl
from jax.experimental.pallas import tpu as pltpu
from jax.sharding import PartitionSpec as P

MESH = pl.DeviceIdType.MESH
F32 = jnp.float32
BF16 = jnp.bfloat16

WIDTH = 1376
CHUNKS = ((0, 512, 512), (512, 512, 512), (1024, 352, 384))
HALF = 256
SLOT = 1408
ORDER = (
    "C", "P0", "P1", "P2", "D", "C", "S0", "S1", "S2", "D", "C", "M0", "M1", "M2", "D", "C", "G0",
    "G1", "G2", "D", "C", "H0", "H1", "H2", "U0", "D", "C", "U1", "U2", "D", "C", "F0", "F1", "D",
    "C", "F2", "E0", "E1", "D", "E2",
)


def pack(rows):
    low, high = rows[:, :HALF], rows[:, HALF:]
    if high.shape[1] < HALF:
        high = jnp.concatenate(
            [high, jnp.zeros((8, HALF - high.shape[1]), high.dtype)], axis=1
        )
    return jnp.concatenate([low, high], axis=0)


def unpack(block):
    return jnp.concatenate([block[:8], block[8:]], axis=1)


def kernel(
    grad_ref, hidden_ref, basis_ref, weight_ref, first_ref, second_ref,
    slots_ref, new_first_ref, new_second_ref,
    grad, hidden, basis, weight, first, second, load_sem,
    gathered, expand, proj, dirs,
    part0, part1, part2, ra0, ra1, ra2, sz, rz, steps, local_new, own_sem,
    a_send, a_recv, p_send, p_recv, c_send, c_recv,
):
    parts, ras = (part0, part1, part2), (ra0, ra1, ra2)
    dp, tensor = lax.axis_index("dp"), lax.axis_index("tensor")
    y, x, z = dp // 16, (dp // 4) % 4, dp % 4
    hi, core = tensor // 2, tensor % 2
    even = core == 0
    a, b = jnp.where(even, y, x), jnp.where(even, x, y)

    def device(a_, b_, z_, hi_, core_):
        y_, x_ = jnp.where(even, a_, b_), jnp.where(even, b_, a_)
        return ((y_ * 4 + x_) * 4 + z_, hi_ * 2 + core_)

    a_peers = [device((a + k) % 4, b, z, hi, core) for k in (1, 2, 3)]
    b_peers = [device(a, (b + k) % 4, z, hi, core) for k in (1, 2, 3)]
    z_peers = [device(a, b, (z + k) % 4, hi, core) for k in (1, 2, 3)]
    hi_next = device(a, b, z, (hi + 1) % 4, core)
    hi_prev = device(a, b, z, (hi + 3) % 4, core)
    sibling = (dp, hi * 2 + 1 - core)

    loads = [
        pltpu.make_async_copy(basis_ref, basis, load_sem.at[0]),
        pltpu.make_async_copy(grad_ref, grad, load_sem.at[1]),
        pltpu.make_async_copy(hidden_ref, hidden.at[pl.ds(0, WIDTH)], load_sem.at[2]),
        pltpu.make_async_copy(first_ref, first, load_sem.at[3]),
        pltpu.make_async_copy(second_ref, second, load_sem.at[4]),
        pltpu.make_async_copy(weight_ref, weight, load_sem.at[5]),
    ]
    for load in loads:
        load.start()

    barrier = pltpu.get_barrier_semaphore()
    friends = a_peers + b_peers + z_peers + [hi_next, hi_prev, sibling]
    for friend in friends:
        pl.semaphore_signal(barrier, inc=1, device_id=friend, device_id_type=MESH)

    sends = []

    def send(src, dst, send_sem, recv_sem, to):
        copy = pltpu.make_async_remote_copy(
            src_ref=src, dst_ref=dst, send_sem=send_sem, recv_sem=recv_sem,
            device_id=to, device_id_type=MESH,
        )
        copy.start()
        sends.append(copy)
        return copy

    hidden[pl.ds(WIDTH, SLOT - WIDTH)] = jnp.zeros((SLOT - WIDTH, 256), BF16)
    dirs[...] = jnp.zeros_like(dirs)
    loads[0].wait()
    mine = a * 16 + b * 4 + z
    columns = pl.ds(pl.multiple_of(core * 256, 256), 256)
    gathered[mine] = basis[:, columns]
    pl.semaphore_wait(barrier, len(friends))

    near = (2, 1, 3)
    arrivals = {}

    def pass_on(kb, kz, axes):
        at = gathered.at[a * 16 + (b + 4 - kb) % 4 * 4 + (z + 4 - kz) % 4]
        for axis in axes:
            for k in near:
                if axis == "z":
                    index, to, key = k - 1, z_peers[k - 1], (0, 0, k)
                elif axis == "b":
                    index, to, key = 3 + kz * 3 + k - 1, b_peers[k - 1], (0, k, kz)
                else:
                    index, to, key = 15 + (kb * 4 + kz) * 3 + k - 1, a_peers[k - 1], (k, kb, kz)
                arrivals[key] = send(at, at, a_send.at[index], a_recv.at[index], to)

    pass_on(0, 0, "zba")
    for kz in near:
        arrivals[0, 0, kz].wait_recv()
        pass_on(0, kz, "ba")
    for kz in (0,) + near:
        for kb in near:
            arrivals[0, kb, kz].wait_recv()
            pass_on(kb, kz, "a")

    lane = lax.broadcasted_iota(jnp.int32, (1, 1024), 1)
    la, lb = lane // 256, (lane // 64) % 4
    rank = jnp.where(even, la * 4 + lb, lb * 4 + la) * 32 + (lane // 16 % 4) * 8 + lane % 8
    row = lax.broadcasted_iota(jnp.int32, (512, 1024), 0)
    spread = jnp.dot(
        basis[...], jnp.where(row == rank, 1.0, 0.0).astype(BF16), preferred_element_type=F32
    )
    lower = lane // 8 % 2 == 0
    expand[0] = jnp.where(lower, spread, 0.0).astype(BF16)
    expand[1] = jnp.where(lower, 0.0, spread).astype(BF16)
    loads[1].wait()

    total = jnp.zeros((256, 256), F32)
    for kb in (0,) + near:
        for ka in (0,) + near:
            if ka:
                for kz in range(4):
                    arrivals[ka, kb, kz].wait_recv()
            a_, b_ = (a + 4 - ka) % 4, (b + 4 - kb) % 4
            at = pl.multiple_of(jnp.where(even, a_ * 4 + b_, b_ * 4 + a_) * 256, 256)
            rows = gathered[pl.ds(a_ * 16 + b_ * 4, 4)].reshape(256, 256)
            total += jnp.dot(grad[:, pl.ds(at, 256)], rows, preferred_element_type=F32)
    proj[core] = total.T.astype(BF16)
    half = send(proj.at[core], proj.at[core], p_send, p_recv, sibling)
    loads[2].wait()
    half.wait_recv()
    for load in loads[3:]:
        load.wait()

    waits = {}

    def stage_partial(c):
        first_column, _, padded = CHUNKS[c]
        for h in range(2):
            part = lax.dot_general(
                proj[h], hidden[pl.ds(first_column, padded)],
                (((1,), (1,)), ((), ())), preferred_element_type=F32,
            )
            for i in range(8):
                y_, x_ = (h * 8 + i) // 4, i % 4
                parts[c][jnp.where(even, y_ * 4 + x_, x_ * 4 + y_)] = part[i * 32 : i * 32 + 32].astype(BF16)
        waits["a", c] = [
            send(parts[c].at[pl.ds((a + k + 1) % 4 * 4, 4)], ras[c].at[k], c_send.at[c, k], c_recv.at[c, k], a_peers[k])
            for k in (1, 0, 2)
        ]

    def stage_sum_a(c):
        for copy in waits["a", c]:
            copy.wait_recv()
        total = parts[c][pl.ds(a * 4, 4)].astype(F32)
        for k in range(3):
            total += ras[c][k].astype(F32)
        for b_ in range(4):
            for z_ in range(4):
                sz[c, b_ * 4 + z_] = pack(total[b_, z_ * 8 : z_ * 8 + 8]).astype(BF16)
        waits["bz", c] = [
            send(sz.at[c, (b + kb) % 4 * 4 + (z + kz) % 4], rz.at[c, kb * 4 + kz],
                 c_send.at[c, 2 + kb * 4 + kz], c_recv.at[c, 2 + kb * 4 + kz], device(a, (b + kb) % 4, (z + kz) % 4, hi, core))
            for kb in (2, 1, 3, 0) for kz in (3, 2, 1, 0) if kb or kz
        ]

    def stage_moments(c):
        first_column, valid, _ = CHUNKS[c]
        at = pl.ds(first_column, valid)
        total = sz[c, b * 4 + z].astype(F32)
        for copy in waits["bz", c]:
            copy.wait_recv()
        for k in range(1, 16):
            total += rz[c, k].astype(F32)
        grad_low = unpack(total)[:, :valid]
        new_first = 0.9 * first[:, at] + 0.1 * grad_low
        new_second = 0.999 * second[:, at] + 0.001 * grad_low * grad_low
        new_first_ref[:, at] = new_first
        new_second_ref[:, at] = new_second
        dirs[:, at] = new_first / (jnp.sqrt(new_second) + 1e-08)
        steps[c, mine] = pack(dirs[:, pl.ds(first_column, 512)]).astype(BF16)
        waits["gz", c] = [
            send(steps.at[c, mine], steps.at[c, mine], c_send.at[c, 18 + k], c_recv.at[c, 18 + k], z_peers[k])
            for k in range(3)
        ]

    def spread_a(c, kb):
        block = steps.at[c, pl.ds(a * 16 + (b + 4 - kb) % 4 * 4, 4)]
        waits["ga", c] += [
            send(block, block, c_send.at[c, 23 + kb * 3 + k], c_recv.at[c, 23 + kb * 3 + k], a_peers[k - 1]) for k in near
        ]

    def stage_gather(c):
        for copy in waits["gz", c]:
            copy.wait_recv()
        block = steps.at[c, pl.ds(a * 16 + b * 4, 4)]
        waits["gb", c] = {
            k: send(block, block, c_send.at[c, 20 + k], c_recv.at[c, 20 + k], b_peers[k - 1]) for k in near
        }
        waits["ga", c] = []
        spread_a(c, 0)

    def stage_hand_on(c):
        for kb in near:
            waits["gb", c][kb].wait_recv()
            spread_a(c, kb)

    def slot(c, hi_, core_, rows=pl.ds(0, 64)):
        return slots_ref.at[hi_ * 2 + core_, rows, pl.ds(CHUNKS[c][0], CHUNKS[c][2])]

    top, bottom = pl.ds(0, 32), pl.ds(32, 32)
    own = []

    def stage_update(c):
        first_column, valid, padded = CHUNKS[c]
        for copy in waits["ga", c]:
            copy.wait_recv()
        every = steps[c].reshape(1024, HALF)
        update = jnp.concatenate(
            [jnp.dot(expand[h], every, preferred_element_type=F32) for h in range(2)], axis=1
        )[:, :valid]
        new = weight[:, pl.ds(first_column, valid)].astype(F32) - 0.1 * update
        local_new[:, pl.ds(first_column, valid)] = new.astype(BF16)
        src = local_new.at[:, pl.ds(first_column, padded)]
        waits["n", c] = send(src, slot(c, hi, core), c_send.at[c, 36], c_recv.at[c, 36], hi_next)
        waits["p", c] = send(src, slot(c, hi, core), c_send.at[c, 37], c_recv.at[c, 37], hi_prev)
        waits["s", c] = send(src, slot(c, hi, core), c_send.at[c, 38], c_recv.at[c, 38], sibling)
        copy = pltpu.make_async_copy(src, slot(c, hi, core), own_sem.at[c])
        copy.start()
        own.append(copy)

    def stage_forward(c):
        waits["n", c].wait_recv()
        prev = (hi + 3) % 4
        waits["n2", c] = send(slot(c, prev, core, top), slot(c, prev, core, top), c_send.at[c, 39], c_recv.at[c, 39], hi_next)
        waits["ns", c] = send(slot(c, prev, core), slot(c, prev, core), c_send.at[c, 40], c_recv.at[c, 40], sibling)
        waits["p", c].wait_recv()
        following = (hi + 1) % 4
        waits["p2", c] = send(slot(c, following, core, bottom), slot(c, following, core, bottom), c_send.at[c, 41], c_recv.at[c, 41], hi_prev)
        waits["ps", c] = send(slot(c, following, core), slot(c, following, core), c_send.at[c, 42], c_recv.at[c, 42], sibling)

    def stage_finish(c):
        far = (hi + 2) % 4
        waits["n2", c].wait_recv()
        waits["fs", c] = send(slot(c, far, core, top), slot(c, far, core, top), c_send.at[c, 43], c_recv.at[c, 43], sibling)
        waits["p2", c].wait_recv()
        waits["gs", c] = send(slot(c, far, core, bottom), slot(c, far, core, bottom), c_send.at[c, 44], c_recv.at[c, 44], sibling)

    stages = dict(
        P=stage_partial, S=stage_sum_a, M=stage_moments, G=stage_gather, H=stage_hand_on, U=stage_update, F=stage_forward, E=stage_finish
    )
    drained = 0
    for item in ORDER:
        if item == "D":
            for copy in sends[drained:checked]:
                copy.wait_send()
            drained = checked
        elif item == "C":
            checked = len(sends)
        else:
            stages[item[0]](int(item[1]))
    n = len(CHUNKS)
    for c in range(n):
        for name in ("s", "ns", "ps", "fs", "gs"):
            waits[name, c].wait_recv()
    for copy in own:
        copy.wait()
    for copy in sends[drained:]:
        copy.wait_send()


def assemble(slots_ref, first_ref, second_ref, weight_ref, new_first_ref, new_second_ref):
    for t in range(8):
        weight_ref[:, WIDTH * t : WIDTH * (t + 1)] = slots_ref[t, :, :WIDTH]
    new_first_ref[...] = first_ref[...]
    new_second_ref[...] = second_ref[...]


def local(grad_out, hidden, proj_basis, weight, first_moment, second_moment):
    n = len(CHUNKS)
    wide = [padded for _, _, padded in CHUNKS]
    hbm = pl.BlockSpec(memory_space=pl.ANY)
    vmem = pl.BlockSpec(memory_space=pltpu.VMEM)
    dma = pltpu.SemaphoreType.DMA
    slots, new_first, new_second = pl.pallas_call(
        kernel,
        name="step",
        out_shape=(
            jax.ShapeDtypeStruct((8, 64, SLOT), BF16),
            jax.ShapeDtypeStruct((8, WIDTH), F32),
            jax.ShapeDtypeStruct((8, WIDTH), F32),
        ),
        in_specs=[hbm] * 6,
        out_specs=(hbm, vmem, vmem),
        scratch_shapes=[
            pltpu.VMEM((256, 4096), BF16),
            pltpu.VMEM((SLOT, 256), BF16),
            pltpu.VMEM((64, 512), BF16),
            pltpu.VMEM((64, WIDTH), BF16),
            pltpu.VMEM((8, WIDTH), F32),
            pltpu.VMEM((8, WIDTH), F32),
            dma((6,)),
            pltpu.VMEM((64, 64, 256), BF16),
            pltpu.VMEM((2, 64, 1024), BF16),
            pltpu.VMEM((2, 256, 256), BF16),
            pltpu.VMEM((8, 1536), F32),
            *[pltpu.VMEM((16, 32, w), BF16) for w in wide],
            *[pltpu.VMEM((3, 4, 32, w), BF16) for w in wide],
            pltpu.VMEM((n, 16, 16, HALF), BF16),
            pltpu.VMEM((n, 16, 16, HALF), BF16),
            pltpu.VMEM((n, 64, 16, HALF), BF16),
            pltpu.VMEM((64, SLOT), BF16),
            dma((n,)),
            dma((63,)), dma((63,)), dma, dma, dma((n, 45)), dma((n, 45)),
        ],
        compiler_params=pltpu.CompilerParams(
            collective_id=0, has_side_effects=True, vmem_limit_bytes=62 * 2**20
        ),
    )(grad_out, hidden.T, proj_basis, weight, first_moment, second_moment)
    moments = pl.BlockSpec((8, WIDTH), lambda i: (0, 0))
    return pl.pallas_call(
        assemble,
        name="assemble",
        grid=(2,),
        out_shape=(
            jax.ShapeDtypeStruct((64, 8 * WIDTH), BF16),
            jax.ShapeDtypeStruct((8, WIDTH), F32),
            jax.ShapeDtypeStruct((8, WIDTH), F32),
        ),
        in_specs=[pl.BlockSpec((8, 32, SLOT), lambda i: (0, i, 0)), moments, moments],
        out_specs=(pl.BlockSpec((32, 8 * WIDTH), lambda i: (i, 0)), moments, moments),
        compiler_params=pltpu.CompilerParams(vmem_limit_bytes=62 * 2**20),
    )(slots, new_first, new_second)


def solution(mesh):
    return jax.shard_map(
        local,
        mesh=mesh,
        in_specs=(
            P("dp", None),
            P("dp", "tensor"),
            P("dp", None),
            P("dp", "tensor"),
            P("dp", "tensor"),
            P("dp", "tensor"),
        ),
        out_specs=(P("dp", None), P("dp", "tensor"), P("dp", "tensor")),
        check_vma=False,
    )
```
